32 devices in a mesh: groups: 2 (over y), cols: 4 (over z), rows: 2 (over x), pair: 2 (over core).
Axes of the slice: x: 2, y: 2, z: 4, core: 2. Of those that a mesh axis runs over, the one named last changes fastest.
Arguments:
- clip_inputs: bfloat16 [2, 512, 1024], P(None, 'groups', 'rows'), parts along dimension 1, may hold values from -6 to 6
- head_weights: bfloat16 [2, 1024, 1024], P(None, 'rows', 'cols'), may hold values from -0.1875 to 0.1875
- owner_slot: int32 [512], P('groups'), parts along dimension 0, may hold values from 0 to 255, each once
- sign_seed: int32 [1], replicated, may hold values from 0 to 1073741823
Outputs:
- features: float32 [512, 1024], P(('groups', 'cols', 'rows'), 'pair'), parts along dimension 0
The draws below stay inside these ranges and needn't reach their ends.
There are 2 independent parts, one for each index of `groups`. The reference program is written for one: setup_inputs(seed, part) draws one part's arguments, and reference() takes and returns one part's arrays. A program takes and returns all parts, laid end to end along the dimension named above; an argument that names none is the same for every part. Nothing has to cross between parts.
Inputs may be any that keep to these rules, and one draw needn't show every extreme that they name: `owner_slot`: each of 0 to 255 appears exactly once.
All inputs are finite; a program needn't handle non-finite values.
Results may differ from the reference program's by a relative error of at most 0.0029.
Values sent between devices are 32-bit elements; how exact they have to be, the bound alone decides.
A program may use at most 64 MiB of HBM per device.

```python
import jax
import jax.numpy as jnp
from jax import lax

D = 1024
PROJ = 1024
CLIPS = 256


def shard_levels(key, extent, pieces, low, high):
    factor_of = 1.0
    for axis_at, blocks in pieces:
        draws = jax.random.uniform(jax.random.fold_in(jax.random.fold_in(key, 6), axis_at), (blocks,), jnp.float32, low / len(pieces), high / len(pieces))
        factor_of = factor_of * jnp.repeat(jnp.exp(draws), extent[axis_at] // blocks).reshape((-1,) + (1,) * (len(extent) - 1 - axis_at))
    return factor_of


def noise(stream_key, shape, scale, most, split=(), kind=jnp.bfloat16):
    array = scale * jax.random.normal(stream_key, shape, jnp.float32)
    if split:
        array = array * shard_levels(stream_key, shape, split, -0.22, 0.18)
    return jnp.clip(array, -most, most).astype(kind)


def setup_inputs(seed: int = 0, part: int = 0) -> dict:
    seeds = jax.random.split(jax.random.key(seed), 5)
    part_splits = jax.random.split(jax.random.fold_in(seeds[4], part), 5)
    return {
        "clip_inputs": noise(part_splits[0], (2, CLIPS, D), 1.0, 6.0, ((2, 2),)),
        "head_weights": noise(seeds[1], (2, D, D), D ** -0.5, 0.1875, ((1, 2), (2, 4))),
        "owner_slot": jax.random.permutation(part_splits[2], CLIPS).astype(jnp.int32),
        "sign_seed": jax.random.randint(seeds[3], (1,), 0, 1073741824).astype(jnp.int32),
    }


logit_scale = 14.0

def sign_values(seed_value, k_index, a_index, b_index, full_width):
    m_index = jnp.arange(2, dtype=jnp.int32).reshape(2, 1, 1, 1)
    k_grid = k_index.astype(jnp.int32).reshape(1, 1, -1, 1)
    a_grid = a_index.astype(jnp.int32).reshape(1, -1, 1, 1)
    b_grid = b_index.astype(jnp.int32).reshape(1, 1, 1, -1)
    width = jnp.int32(full_width)
    mixer = jnp.int32(73244475)
    golden = jnp.int32(-1640531535)
    numbers = ((k_grid * 2 + m_index) * width + a_grid) * width + b_grid
    hashed = numbers + seed_value.astype(jnp.int32) * golden
    hashed = hashed * mixer
    hashed = hashed ^ lax.shift_right_logical(hashed, jnp.int32(16))
    hashed = hashed * mixer
    hashed = hashed ^ lax.shift_right_logical(hashed, jnp.int32(16))
    low_bit = lax.shift_right_logical(hashed, jnp.int32(8)) & jnp.int32(1)
    return (1.0 - 2.0 * low_bit.astype(jnp.float32)) * full_width ** (-0.5)

def head_grads(embedded):
    inv_norm = 1.0 / jnp.sqrt(lax.optimization_barrier(jnp.sum(embedded * embedded, axis=2, keepdims=True)) + 1e-06)
    unit = embedded * inv_norm
    scores = logit_scale * jnp.dot(unit[0], unit[1].T, precision=lax.Precision.HIGHEST, preferred_element_type=jnp.float32)
    expo = jnp.exp(scores - logit_scale)
    row_soft = expo / lax.optimization_barrier(jnp.sum(expo, axis=1, keepdims=True))
    col_soft = (expo / lax.optimization_barrier(jnp.sum(expo, axis=0, keepdims=True))).T
    own_row = jnp.diagonal(row_soft)[:, None]
    own_col = jnp.diagonal(col_soft)[:, None]
    half_scale = 0.5 * logit_scale
    grad_audio = half_scale * (jnp.dot(row_soft, unit[1], precision=lax.Precision.HIGHEST, preferred_element_type=jnp.float32) - (2.0 - own_col) * unit[1])
    grad_video = half_scale * (jnp.dot(col_soft, unit[0], precision=lax.Precision.HIGHEST, preferred_element_type=jnp.float32) - (2.0 - own_row) * unit[0])
    unit_grad = jnp.stack([grad_audio, grad_video])
    along = lax.optimization_barrier(jnp.sum(unit * unit_grad, axis=2, keepdims=True))
    return ((unit_grad - unit * along) * inv_norm).astype(jnp.bfloat16)

def reference(clip_inputs, head_weights, owner_slot, sign_seed):
    inputs_wide = clip_inputs.astype(jnp.float32)
    embedded = jnp.einsum('mia,mab->mib', inputs_wide, head_weights.astype(jnp.float32), precision=lax.Precision.HIGHEST)
    grads_wide = head_grads(embedded).astype(jnp.float32)
    block_size = min(4, PROJ)
    seed_value = sign_seed[0]
    a_index = jnp.arange(D, dtype=jnp.int32)
    b_index = jnp.arange(D, dtype=jnp.int32)

    def feature_block(block_start):
        k_index = block_start + jnp.arange(block_size, dtype=jnp.int32)
        signs = sign_values(seed_value, k_index, a_index, b_index, D)
        product = jnp.einsum('mia,makb->mikb', inputs_wide, signs, precision=lax.Precision.HIGHEST)
        return jnp.einsum('mikb,mib->ik', product, grads_wide, precision=lax.Precision.HIGHEST)
    starts = jnp.arange(PROJ // block_size, dtype=jnp.int32) * block_size
    blocks = lax.map(feature_block, starts)
    phi = jnp.transpose(blocks, (1, 0, 2)).reshape(CLIPS, PROJ)
    return jnp.zeros((CLIPS, PROJ), jnp.float32).at[owner_slot].set(phi)
```

```python
import functools

import jax
import jax.numpy as jnp
from jax import lax
from jax.experimental import pallas as pl
from jax.experimental.pallas import tpu as pltpu
from jax.sharding import PartitionSpec as P

D = 1024
PROJ = 1024
MIXER = 73244475
GOLDEN = -1640531535
RESIDUES = 16
GROUP = 8

logit_scale = 14.0


def wrap32(value):
    value &= 0xFFFFFFFF
    return value - (1 << 32) if value >= (1 << 31) else value


def shift_right(value, amount):
    return lax.shift_right_logical(value, jnp.full((), amount, value.dtype))


def project_kernel(base_ref, x_ref, g_ref, o_ref, top_ref, low_ref, add_ref, gain_ref, even_ref, odd_ref):
    res = pl.program_id(0)
    m = pl.program_id(1)
    b_part, a_part = top_ref.shape
    steps = o_ref.shape[1]
    i32, i16 = jnp.int32, jnp.int16
    start = base_ref[0] + (res * 2 + m) * i32(D * D)
    rows = 32

    def prepare(step, carry):
        at = pl.ds(pl.multiple_of(step * rows, rows), rows)
        b_index = lax.broadcasted_iota(i32, (rows, a_part), 0) + step * rows
        a_index = lax.broadcasted_iota(i32, (rows, a_part), 1)
        h1 = (start + a_index * D + b_index) * i32(MIXER)
        h2 = h1 ^ shift_right(h1, 16)
        bit8 = shift_right(h2 * i32(MIXER), 8) & 1
        high = shift_right(h1, 16)
        w = high & 0x1FF
        fixed = ((w << 16) | ((h1 & 0x1FF) ^ w)) * i32(MIXER)
        top_ref[at, :] = (high & 0xFE00).astype(i16)
        low_ref[at, :] = (h1 & 0xFE00).astype(i16)
        add_ref[at, :] = (shift_right(fixed, 9) + (bit8 << 15)).astype(i16)
        return carry

    lax.fori_loop(0, b_part // rows, prepare, 0)
    gain_ref[...] = g_ref[m].astype(jnp.float32) * (D**-0.5)

    def fill(ref, step):
        for u in range(GROUP):
            shift = shift_right((step * GROUP + u) * i32(wrap32(MIXER << 25)), 16).astype(i16)
            mixed = shift_right((top_ref[...] + shift) ^ low_ref[...], 9)
            value = mixed * i16((MIXER & 0xFFFF) - 0x10000) + add_ref[...]
            ref[u * b_part : (u + 1) * b_part, :] = jnp.where(value < 0, jnp.bfloat16(-1), jnp.bfloat16(1))

    def use(ref, step):
        product = jnp.dot(ref[...], x_ref[m], preferred_element_type=jnp.float32)
        n = product.shape[1]
        terms = product.reshape(GROUP, b_part // 8, 8, n) * gain_ref[...].reshape(1, b_part // 8, 8, n)
        total = jnp.sum(jnp.sum(terms, axis=1), axis=1)
        o_ref[res, step] = jnp.where(m == 0, 0.0, o_ref[res, step]) + total

    fill(even_ref, 0)

    def body(t, carry):
        use(even_ref, 2 * t)
        fill(odd_ref, 2 * t + 1)
        use(odd_ref, 2 * t + 1)
        fill(even_ref, 2 * t + 2)
        return carry

    lax.fori_loop(0, steps // 2, body, 0)


def project(base, x, g, k_count):
    _, a_part, n = x.shape
    b_part = g.shape[1]
    steps = k_count // (RESIDUES * GROUP)
    whole = pl.BlockSpec(memory_space=pltpu.VMEM)
    return pl.pallas_call(
        project_kernel,
        grid=(RESIDUES, 2),
        in_specs=[pl.BlockSpec(memory_space=pltpu.SMEM), whole, whole],
        out_specs=whole,
        out_shape=jax.ShapeDtypeStruct((RESIDUES, steps, GROUP, n), jnp.float32),
        scratch_shapes=[pltpu.VMEM((b_part, a_part), jnp.int16)] * 3
        + [pltpu.VMEM((b_part, n), jnp.float32)]
        + [pltpu.VMEM((GROUP * b_part, a_part), jnp.bfloat16)] * 2,
        compiler_params=pltpu.CompilerParams(vmem_limit_bytes=48 * 2**20),
    )(base, x, g)


def head_grads(embedded):
    clips = embedded.shape[2]
    exact = dict(precision=lax.Precision.HIGHEST, preferred_element_type=jnp.float32)
    raw = lax.dot_general(embedded[0], embedded[1], (((0,), (0,)), ((), ())), **exact)
    squares = jnp.sum(embedded * embedded, axis=1)
    both = lax.psum(jnp.concatenate([raw, squares], axis=0), "cols")
    inv_norm = 1.0 / jnp.sqrt(both[clips:] + 1e-06)
    unit = embedded * inv_norm[:, None, :]
    cosine = both[:clips] * inv_norm[0][:, None] * inv_norm[1][None, :]
    expo = jnp.exp(logit_scale * cosine - logit_scale)
    row_soft = expo / jnp.sum(expo, axis=1, keepdims=True)
    col_soft = expo / jnp.sum(expo, axis=0, keepdims=True)
    rest_row = 2.0 - jnp.diagonal(row_soft)
    rest_col = 2.0 - jnp.diagonal(col_soft)
    own = jnp.diagonal(cosine)
    half_scale = 0.5 * logit_scale
    pull_audio = lax.dot_general(unit[1], row_soft, (((1,), (1,)), ((), ())), **exact)
    pull_video = lax.dot_general(unit[0], col_soft, (((1,), (0,)), ((), ())), **exact)
    unit_grad = half_scale * jnp.stack([pull_audio - rest_col * unit[1], pull_video - rest_row * unit[0]])
    along_audio = jnp.sum(row_soft * cosine, axis=1) - rest_col * own
    along_video = jnp.sum(col_soft * cosine, axis=0) - rest_row * own
    along = half_scale * jnp.stack([along_audio, along_video])[:, None, :]
    return ((unit_grad - unit * along) * inv_norm[:, None, :]).astype(jnp.bfloat16)


def per_device(clip_inputs, head_weights, owner_slot, sign_seed):
    clip_count = clip_inputs.shape[1]
    a_part = clip_inputs.shape[2]
    b_part = head_weights.shape[2]
    k_part = PROJ // lax.axis_size("pair")
    a_start = lax.axis_index("rows") * a_part
    b_start = lax.axis_index("cols") * b_part
    k_start = lax.axis_index("pair") * k_part
    slots = jnp.arange(clip_count, dtype=jnp.int32)
    chosen = (owner_slot[None, :] == slots[:, None]).astype(jnp.bfloat16)
    x = jnp.einsum("mia,si->mas", clip_inputs, chosen, preferred_element_type=jnp.float32).astype(jnp.bfloat16)
    partial_value = jnp.einsum("mab,mas->mbs", head_weights, x, preferred_element_type=jnp.float32)
    grads = head_grads(lax.psum(partial_value, "rows"))
    base = sign_seed * jnp.int32(GOLDEN) + (k_start * (2 * D * D) + a_start * D + b_start).astype(jnp.int32)
    phi = project(base, x, grads, k_part)
    phi = jnp.transpose(phi.reshape(RESIDUES, -1, clip_count), (2, 1, 0)).reshape(clip_count, k_part)
    return lax.psum_scatter(phi, ("cols", "rows"), scatter_dimension=0, tiled=True)


def solution(mesh):
    placed = (P(None, "groups", "rows"), P(None, "rows", "cols"), P("groups"), P())
    return jax.shard_map(
        per_device,
        mesh=mesh,
        in_specs=placed,
        out_specs=P(("groups", "cols", "rows"), "pair"),
        check_vma=False,
    )
```

```python
import functools

import jax
import jax.numpy as jnp
from jax import lax
from jax.experimental import pallas as pl
from jax.experimental.pallas import tpu as pltpu
from jax.sharding import PartitionSpec as P

D = 1024
PROJ = 1024
MIXER = 73244475
GOLDEN = -1640531535
RESIDUES = 16
GROUP = 8

logit_scale = 14.0


def wrap32(value):
    value &= 0xFFFFFFFF
    return value - (1 << 32) if value >= (1 << 31) else value


def shift_right(value, amount):
    return lax.shift_right_logical(value, jnp.full((), amount, value.dtype))


def project_kernel(base_ref, x_ref, g_ref, o_ref, top_ref, low_ref, add_ref, gain_ref, even_ref, odd_ref):
    res = pl.program_id(0)
    m = pl.program_id(1)
    b_part, a_part = top_ref.shape
    steps = o_ref.shape[1]
    i32, i16 = jnp.int32, jnp.int16
    start = base_ref[0] + (res * 2 + m) * i32(D * D)
    rows = 32

    def prepare(step, carry):
        at = pl.ds(pl.multiple_of(step * rows, rows), rows)
        b_index = lax.broadcasted_iota(i32, (rows, a_part), 0) + step * rows
        a_index = lax.broadcasted_iota(i32, (rows, a_part), 1)
        h1 = (start + a_index * D + b_index) * i32(MIXER)
        h2 = h1 ^ shift_right(h1, 16)
        bit8 = shift_right(h2 * i32(MIXER), 8) & 1
        high = shift_right(h1, 16)
        w = high & 0x1FF
        fixed = ((w << 16) | ((h1 & 0x1FF) ^ w)) * i32(MIXER)
        top_ref[at, :] = (high & 0xFE00).astype(i16)
        low_ref[at, :] = (h1 & 0xFE00).astype(i16)
        add_ref[at, :] = (shift_right(fixed, 9) + (bit8 << 15)).astype(i16)
        return carry

    lax.fori_loop(0, b_part // rows, prepare, 0)
    gain_ref[...] = g_ref[m].astype(jnp.float32) * (D**-0.5)

    def fill(ref, step):
        for u in range(GROUP):
            shift = shift_right((step * GROUP + u) * i32(wrap32(MIXER << 25)), 16).astype(i16)
            mixed = shift_right((top_ref[...] + shift) ^ low_ref[...], 9)
            value = mixed * i16((MIXER & 0xFFFF) - 0x10000) + add_ref[...]
            ref[u * b_part : (u + 1) * b_part, :] = jnp.where(value < 0, jnp.bfloat16(-1), jnp.bfloat16(1))

    def use(ref, step):
        product = jnp.dot(ref[...], x_ref[m], preferred_element_type=jnp.float32)
        n = product.shape[1]
        terms = product.reshape(GROUP, b_part // 8, 8, n) * gain_ref[...].reshape(1, b_part // 8, 8, n)
        total = jnp.sum(jnp.sum(terms, axis=1), axis=1)
        o_ref[res, step] = jnp.where(m == 0, 0.0, o_ref[res, step]) + total

    fill(even_ref, 0)

    def body(t, carry):
        use(even_ref, 2 * t)
        fill(odd_ref, 2 * t + 1)
        use(odd_ref, 2 * t + 1)
        fill(even_ref, 2 * t + 2)
        return carry

    lax.fori_loop(0, steps // 2, body, 0)


def project(base, x, g, k_count):
    _, a_part, n = x.shape
    b_part = g.shape[1]
    steps = k_count // (RESIDUES * GROUP)
    whole = pl.BlockSpec(memory_space=pltpu.VMEM)
    return pl.pallas_call(
        project_kernel,
        grid=(RESIDUES, 2),
        in_specs=[pl.BlockSpec(memory_space=pltpu.SMEM), whole, whole],
        out_specs=whole,
        out_shape=jax.ShapeDtypeStruct((RESIDUES, steps, GROUP, n), jnp.float32),
        scratch_shapes=[pltpu.VMEM((b_part, a_part), jnp.int16)] * 3
        + [pltpu.VMEM((b_part, n), jnp.float32)]
        + [pltpu.VMEM((GROUP * b_part, a_part), jnp.bfloat16)] * 2,
        compiler_params=pltpu.CompilerParams(vmem_limit_bytes=48 * 2**20),
    )(base, x, g)


MESH = pl.DeviceIdType.MESH


def sum_kernel(axis, size, part_ref, o_ref, slots_ref, send_sem, recv_sem, swap_send, swap_recv):
    me = lax.axis_index(axis)
    half = lax.axis_index("pair")
    peers = [lax.rem(me + offset, size) for offset in range(1, size)]
    barrier = pltpu.get_barrier_semaphore()
    for peer in peers:
        pl.semaphore_signal(barrier, inc=1, device_id={axis: peer}, device_id_type=MESH)
    pl.semaphore_signal(barrier, inc=1, device_id={"pair": 1 - half}, device_id_type=MESH)
    pl.semaphore_wait(barrier, size)
    copies = []
    for at, peer in enumerate(peers):
        copy = pltpu.make_async_remote_copy(
            src_ref=part_ref.at[half],
            dst_ref=slots_ref.at[at],
            send_sem=send_sem.at[at],
            recv_sem=recv_sem.at[at],
            device_id={axis: peer},
            device_id_type=MESH,
        )
        copy.start()
        copies.append(copy)
    total = part_ref[half]
    for at, copy in enumerate(copies):
        copy.wait()
        total = total + slots_ref[at]
    o_ref[half] = total
    swap = pltpu.make_async_remote_copy(
        src_ref=o_ref.at[half],
        dst_ref=o_ref.at[half],
        send_sem=swap_send,
        recv_sem=swap_recv,
        device_id={"pair": 1 - half},
        device_id_type=MESH,
    )
    swap.start()
    swap.wait()


def sum_over(part, axis, collective_id):
    size = lax.axis_size(axis)
    _, height, n = part.shape
    whole = pl.BlockSpec(memory_space=pltpu.VMEM)
    return pl.pallas_call(
        functools.partial(sum_kernel, axis, size),
        in_specs=[whole],
        out_specs=whole,
        out_shape=jax.ShapeDtypeStruct(part.shape, jnp.float32),
        scratch_shapes=[
            pltpu.VMEM((size - 1, height, n), jnp.float32),
            pltpu.SemaphoreType.DMA((size - 1,)),
            pltpu.SemaphoreType.DMA((size - 1,)),
            pltpu.SemaphoreType.DMA,
            pltpu.SemaphoreType.DMA,
        ],
        compiler_params=pltpu.CompilerParams(
            collective_id=collective_id, has_side_effects=True, vmem_limit_bytes=32 * 2**20
        ),
    )(part)


def scatter_kernel(cols, rows, phi_ref, o_ref, slots_ref, send_sem, recv_sem):
    size = cols * rows
    me = lax.axis_index("cols") * rows + lax.axis_index("rows")
    peers = [lax.rem(me + offset, size) for offset in range(1, size)]
    places = [{"cols": lax.div(peer, rows), "rows": lax.rem(peer, rows)} for peer in peers]
    barrier = pltpu.get_barrier_semaphore()
    for place in places:
        pl.semaphore_signal(barrier, inc=1, device_id=place, device_id_type=MESH)
    pl.semaphore_wait(barrier, size - 1)
    copies = []
    for at, peer in enumerate(peers):
        copy = pltpu.make_async_remote_copy(
            src_ref=phi_ref.at[peer],
            dst_ref=slots_ref.at[at],
            send_sem=send_sem.at[at],
            recv_sem=recv_sem.at[at],
            device_id=places[at],
            device_id_type=MESH,
        )
        copy.start()
        copies.append(copy)
    total = phi_ref[me]
    for at, copy in enumerate(copies):
        copy.wait()
        total = total + slots_ref[at]
    o_ref[...] = total


def scatter_sum(phi, collective_id):
    cols, rows = lax.axis_size("cols"), lax.axis_size("rows")
    size = cols * rows
    _, per, width = phi.shape
    whole = pl.BlockSpec(memory_space=pltpu.VMEM)
    return pl.pallas_call(
        functools.partial(scatter_kernel, cols, rows),
        in_specs=[whole],
        out_specs=whole,
        out_shape=jax.ShapeDtypeStruct((per, width), jnp.float32),
        scratch_shapes=[
            pltpu.VMEM((size - 1, per, width), jnp.float32),
            pltpu.SemaphoreType.DMA((size - 1,)),
            pltpu.SemaphoreType.DMA((size - 1,)),
        ],
        compiler_params=pltpu.CompilerParams(
            collective_id=collective_id, has_side_effects=True, vmem_limit_bytes=32 * 2**20
        ),
    )(phi)


def head_grads(embedded):
    clips = embedded.shape[2]
    exact = dict(precision=lax.Precision.HIGHEST, preferred_element_type=jnp.float32)
    raw = lax.dot_general(embedded[0], embedded[1], (((0,), (0,)), ((), ())), **exact)
    squares = jnp.sum(embedded * embedded, axis=1)
    half = -(-(clips + 2) // 16) * 8
    rest = jnp.zeros((2 * half - clips - 2, clips), jnp.float32)
    packed = jnp.concatenate([raw, squares, rest], axis=0).reshape(2, half, clips)
    both = sum_over(packed, "cols", 1).reshape(2 * half, clips)
    inv_norm = 1.0 / jnp.sqrt(both[clips : clips + 2] + 1e-06)
    unit = embedded * inv_norm[:, None, :]
    cosine = both[:clips] * inv_norm[0][:, None] * inv_norm[1][None, :]
    expo = jnp.exp(logit_scale * cosine - logit_scale)
    row_soft = expo / jnp.sum(expo, axis=1, keepdims=True)
    col_soft = expo / jnp.sum(expo, axis=0, keepdims=True)
    same = jnp.arange(clips)[:, None] == jnp.arange(clips)[None, :]
    rest_row = 2.0 - jnp.sum(jnp.where(same, row_soft, 0.0), axis=0)
    rest_col = 2.0 - jnp.sum(jnp.where(same, col_soft, 0.0), axis=0)
    own = jnp.sum(jnp.where(same, cosine, 0.0), axis=0)
    half_scale = 0.5 * logit_scale
    pull_audio = lax.dot_general(unit[1], row_soft, (((1,), (1,)), ((), ())), **exact)
    pull_video = lax.dot_general(unit[0], col_soft, (((1,), (0,)), ((), ())), **exact)
    unit_grad = half_scale * jnp.stack([pull_audio - rest_col * unit[1], pull_video - rest_row * unit[0]])
    along_audio = jnp.sum(row_soft * cosine, axis=1) - rest_col * own
    along_video = jnp.sum(col_soft * cosine, axis=0) - rest_row * own
    along = half_scale * jnp.stack([along_audio, along_video])[:, None, :]
    return ((unit_grad - unit * along) * inv_norm[:, None, :]).astype(jnp.bfloat16)


def per_device(clip_inputs, head_weights, owner_slot, sign_seed):
    clip_count = clip_inputs.shape[1]
    a_part = clip_inputs.shape[2]
    b_part = head_weights.shape[2]
    k_part = PROJ // lax.axis_size("pair")
    a_start = lax.axis_index("rows") * a_part
    b_start = lax.axis_index("cols") * b_part
    k_start = lax.axis_index("pair") * k_part
    slots = jnp.arange(clip_count, dtype=jnp.int32)
    chosen = (owner_slot[None, :] == slots[:, None]).astype(jnp.bfloat16)
    x = jnp.einsum("mia,si->mas", clip_inputs, chosen, preferred_element_type=jnp.float32).astype(jnp.bfloat16)
    partial_value = jnp.einsum("mab,mas->mbs", head_weights, x, preferred_element_type=jnp.float32)
    grads = head_grads(sum_over(partial_value, "rows", 0))
    base = sign_seed * jnp.int32(GOLDEN) + (k_start * (2 * D * D) + a_start * D + b_start).astype(jnp.int32)
    phi = project(base, x, grads, k_part)
    phi = jnp.transpose(phi.reshape(RESIDUES, -1, clip_count), (2, 1, 0))
    owners = lax.axis_size("cols") * lax.axis_size("rows")
    return scatter_sum(phi.reshape(owners, clip_count // owners, k_part), 2)


def solution(mesh):
    placed = (P(None, "groups", "rows"), P(None, "rows", "cols"), P("groups"), P())
    return jax.shard_map(
        per_device,
        mesh=mesh,
        in_specs=placed,
        out_specs=P(("groups", "cols", "rows"), "pair"),
        check_vma=False,
    )
```

```python
import functools

import jax
import jax.numpy as jnp
from jax import lax
from jax.experimental import pallas as pl
from jax.experimental.pallas import tpu as pltpu
from jax.sharding import PartitionSpec as P

D = 1024
PROJ = 1024
MIXER = 73244475
GOLDEN = -1640531535
RESIDUES = 16
GROUP = 16

logit_scale = 14.0


def wrap32(value):
    value &= 0xFFFFFFFF
    return value - (1 << 32) if value >= (1 << 31) else value


def shift_right(value, amount):
    return lax.shift_right_logical(value, jnp.full((), amount, value.dtype))


def project_kernel(base_ref, x_ref, g_ref, o_ref, top_ref, low_ref, add_ref, gain_ref, sign_ref):
    res = pl.program_id(0)
    m = pl.program_id(1)
    b_part, a_part = top_ref.shape
    steps = o_ref.shape[1]
    i32, i16 = jnp.int32, jnp.int16
    start = base_ref[0] + (res * 2 + m) * i32(D * D)
    rows = 32

    def prepare(step, carry):
        at = pl.ds(pl.multiple_of(step * rows, rows), rows)
        b_index = lax.broadcasted_iota(i32, (rows, a_part), 0) + step * rows
        a_index = lax.broadcasted_iota(i32, (rows, a_part), 1)
        h1 = (start + a_index * D + b_index) * i32(MIXER)
        h2 = h1 ^ shift_right(h1, 16)
        bit8 = shift_right(h2 * i32(MIXER), 8) & 1
        high = shift_right(h1, 16)
        w = high & 0x1FF
        fixed = ((w << 16) | ((h1 & 0x1FF) ^ w)) * i32(MIXER)
        top_ref[at, :] = (high & 0xFE00).astype(i16)
        low_ref[at, :] = (h1 & 0xFE00).astype(i16)
        add_ref[at, :] = (shift_right(fixed, 9) + (bit8 << 15)).astype(i16)
        return carry

    lax.fori_loop(0, b_part // rows, prepare, 0)
    gain_ref[...] = g_ref[m].astype(jnp.float32) * (D**-0.5)

    def fill(ref, step):
        for u in range(GROUP):
            shift = shift_right((step * GROUP + u) * i32(wrap32(MIXER << 25)), 16).astype(i16)
            mixed = shift_right((top_ref[...] + shift) ^ low_ref[...], 9)
            value = mixed * i16((MIXER & 0xFFFF) - 0x10000) + add_ref[...]
            ref[u * b_part : (u + 1) * b_part, :] = jnp.where(value < 0, jnp.bfloat16(-1), jnp.bfloat16(1))

    def use(ref, step):
        product = jnp.dot(ref[...], x_ref[m], preferred_element_type=jnp.float32)
        n = product.shape[1]
        terms = product.reshape(GROUP, b_part // 8, 8, n) * gain_ref[...].reshape(1, b_part // 8, 8, n)
        total = jnp.sum(jnp.sum(terms, axis=1), axis=1)
        o_ref[res, step] = jnp.where(m == 0, 0.0, o_ref[res, step]) + total

    def body(step, carry):
        fill(sign_ref, step)
        use(sign_ref, step)
        return carry

    lax.fori_loop(0, steps, body, 0)


def project(base, x, g, k_count):
    _, a_part, n = x.shape
    b_part = g.shape[1]
    steps = k_count // (RESIDUES * GROUP)
    whole = pl.BlockSpec(memory_space=pltpu.VMEM)
    return pl.pallas_call(
        project_kernel,
        grid=(RESIDUES, 2),
        in_specs=[pl.BlockSpec(memory_space=pltpu.SMEM), whole, whole],
        out_specs=whole,
        out_shape=jax.ShapeDtypeStruct((RESIDUES, steps, GROUP, n), jnp.float32),
        scratch_shapes=[pltpu.VMEM((b_part, a_part), jnp.int16)] * 3
        + [pltpu.VMEM((b_part, n), jnp.float32)]
        + [pltpu.VMEM((GROUP * b_part, a_part), jnp.bfloat16)],
        compiler_params=pltpu.CompilerParams(vmem_limit_bytes=48 * 2**20),
    )(base, x, g)


MESH = pl.DeviceIdType.MESH


def sum_kernel(axis, size, part_ref, o_ref, slots_ref, send_sem, recv_sem, swap_send, swap_recv):
    me = lax.axis_index(axis)
    half = lax.axis_index("pair")
    peers = [lax.rem(me + offset, size) for offset in range(1, size)]
    barrier = pltpu.get_barrier_semaphore()
    for peer in peers:
        pl.semaphore_signal(barrier, inc=1, device_id={axis: peer}, device_id_type=MESH)
    pl.semaphore_signal(barrier, inc=1, device_id={"pair": 1 - half}, device_id_type=MESH)
    pl.semaphore_wait(barrier, size)
    copies = []
    for at, peer in enumerate(peers):
        copy = pltpu.make_async_remote_copy(
            src_ref=part_ref.at[half],
            dst_ref=slots_ref.at[at],
            send_sem=send_sem.at[at],
            recv_sem=recv_sem.at[at],
            device_id={axis: peer},
            device_id_type=MESH,
        )
        copy.start()
        copies.append(copy)
    total = part_ref[half]
    for at, copy in enumerate(copies):
        copy.wait()
        total = total + slots_ref[at]
    o_ref[half] = total
    swap = pltpu.make_async_remote_copy(
        src_ref=o_ref.at[half],
        dst_ref=o_ref.at[half],
        send_sem=swap_send,
        recv_sem=swap_recv,
        device_id={"pair": 1 - half},
        device_id_type=MESH,
    )
    swap.start()
    swap.wait()


def sum_over(part, axis, collective_id):
    size = lax.axis_size(axis)
    _, height, n = part.shape
    whole = pl.BlockSpec(memory_space=pltpu.VMEM)
    return pl.pallas_call(
        functools.partial(sum_kernel, axis, size),
        in_specs=[whole],
        out_specs=whole,
        out_shape=jax.ShapeDtypeStruct(part.shape, jnp.float32),
        scratch_shapes=[
            pltpu.VMEM((size - 1, height, n), jnp.float32),
            pltpu.SemaphoreType.DMA((size - 1,)),
            pltpu.SemaphoreType.DMA((size - 1,)),
            pltpu.SemaphoreType.DMA,
            pltpu.SemaphoreType.DMA,
        ],
        compiler_params=pltpu.CompilerParams(
            collective_id=collective_id, has_side_effects=True, vmem_limit_bytes=32 * 2**20
        ),
    )(part)


def scatter_kernel(cols, rows, phi_ref, o_ref, slots_ref, send_sem, recv_sem):
    size = cols * rows
    me = lax.axis_index("cols") * rows + lax.axis_index("rows")
    peers = [lax.rem(me + offset, size) for offset in range(1, size)]
    places = [{"cols": lax.div(peer, rows), "rows": lax.rem(peer, rows)} for peer in peers]
    barrier = pltpu.get_barrier_semaphore()
    for place in places:
        pl.semaphore_signal(barrier, inc=1, device_id=place, device_id_type=MESH)
    pl.semaphore_wait(barrier, size - 1)
    copies = []
    for at, peer in enumerate(peers):
        copy = pltpu.make_async_remote_copy(
            src_ref=phi_ref.at[peer],
            dst_ref=slots_ref.at[at],
            send_sem=send_sem.at[at],
            recv_sem=recv_sem.at[at],
            device_id=places[at],
            device_id_type=MESH,
        )
        copy.start()
        copies.append(copy)
    total = phi_ref[me]
    for at, copy in enumerate(copies):
        copy.wait()
        total = total + slots_ref[at]
    o_ref[...] = total


def scatter_sum(phi, collective_id):
    cols, rows = lax.axis_size("cols"), lax.axis_size("rows")
    size = cols * rows
    _, per, width = phi.shape
    whole = pl.BlockSpec(memory_space=pltpu.VMEM)
    return pl.pallas_call(
        functools.partial(scatter_kernel, cols, rows),
        in_specs=[whole],
        out_specs=whole,
        out_shape=jax.ShapeDtypeStruct((per, width), jnp.float32),
        scratch_shapes=[
            pltpu.VMEM((size - 1, per, width), jnp.float32),
            pltpu.SemaphoreType.DMA((size - 1,)),
            pltpu.SemaphoreType.DMA((size - 1,)),
        ],
        compiler_params=pltpu.CompilerParams(
            collective_id=collective_id, has_side_effects=True, vmem_limit_bytes=32 * 2**20
        ),
    )(phi)


def head_grads(embedded):
    clips = embedded.shape[2]
    exact = dict(precision=lax.Precision.HIGHEST, preferred_element_type=jnp.float32)
    raw = lax.dot_general(embedded[0], embedded[1], (((0,), (0,)), ((), ())), **exact)
    squares = jnp.sum(embedded * embedded, axis=1)
    half = -(-(clips + 2) // 16) * 8
    rest = jnp.zeros((2 * half - clips - 2, clips), jnp.float32)
    packed = jnp.concatenate([raw, squares, rest], axis=0).reshape(2, half, clips)
    both = sum_over(packed, "cols", 1).reshape(2 * half, clips)
    inv_norm = 1.0 / jnp.sqrt(both[clips : clips + 2] + 1e-06)
    unit = embedded * inv_norm[:, None, :]
    cosine = both[:clips] * inv_norm[0][:, None] * inv_norm[1][None, :]
    expo = jnp.exp(logit_scale * cosine - logit_scale)
    row_soft = expo / jnp.sum(expo, axis=1, keepdims=True)
    col_soft = expo / jnp.sum(expo, axis=0, keepdims=True)
    same = jnp.arange(clips)[:, None] == jnp.arange(clips)[None, :]
    rest_row = 2.0 - jnp.sum(jnp.where(same, row_soft, 0.0), axis=0)
    rest_col = 2.0 - jnp.sum(jnp.where(same, col_soft, 0.0), axis=0)
    own = jnp.sum(jnp.where(same, cosine, 0.0), axis=0)
    half_scale = 0.5 * logit_scale
    pull_audio = lax.dot_general(unit[1], row_soft, (((1,), (1,)), ((), ())), **exact)
    pull_video = lax.dot_general(unit[0], col_soft, (((1,), (0,)), ((), ())), **exact)
    unit_grad = half_scale * jnp.stack([pull_audio - rest_col * unit[1], pull_video - rest_row * unit[0]])
    along_audio = jnp.sum(row_soft * cosine, axis=1) - rest_col * own
    along_video = jnp.sum(col_soft * cosine, axis=0) - rest_row * own
    along = half_scale * jnp.stack([along_audio, along_video])[:, None, :]
    return ((unit_grad - unit * along) * inv_norm[:, None, :]).astype(jnp.bfloat16)


def per_device(clip_inputs, head_weights, owner_slot, sign_seed):
    clip_count = clip_inputs.shape[1]
    a_part = clip_inputs.shape[2]
    b_part = head_weights.shape[2]
    k_part = PROJ // lax.axis_size("pair")
    a_start = lax.axis_index("rows") * a_part
    b_start = lax.axis_index("cols") * b_part
    k_start = lax.axis_index("pair") * k_part
    slots = jnp.arange(clip_count, dtype=jnp.int32)
    chosen = (owner_slot[None, :] == slots[:, None]).astype(jnp.bfloat16)
    x = jnp.einsum("mia,si->mas", clip_inputs, chosen, preferred_element_type=jnp.float32).astype(jnp.bfloat16)
    partial_value = jnp.einsum("mab,mas->mbs", head_weights, x, preferred_element_type=jnp.float32)
    grads = head_grads(sum_over(partial_value, "rows", 0))
    base = sign_seed * jnp.int32(GOLDEN) + (k_start * (2 * D * D) + a_start * D + b_start).astype(jnp.int32)
    phi = project(base, x, grads, k_part)
    phi = jnp.transpose(phi.reshape(RESIDUES, -1, clip_count), (2, 1, 0))
    owners = lax.axis_size("cols") * lax.axis_size("rows")
    return scatter_sum(phi.reshape(owners, clip_count // owners, k_part), 2)


def solution(mesh):
    placed = (P(None, "groups", "rows"), P(None, "rows", "cols"), P("groups"), P())
    return jax.shard_map(
        per_device,
        mesh=mesh,
        in_specs=placed,
        out_specs=P(("groups", "cols", "rows"), "pair"),
        check_vma=False,
    )
```
